512 devices in a mesh: leaf: 32 (over y_lo, z, core), row: 4 (over x), col: 4 (over y_hi).
Axes of the slice: x: 4, y: 8 (y_hi: 4, y_lo: 2; y = y_hi * 2 + y_lo), z: 8, core: 2. Of those that a mesh axis runs over, the one named last changes fastest.
Arguments:
- panel: float32 [131072, 1024], P(('leaf', 'row'), 'col'), may hold values from -1.2 to 1.2
- block_mask: int32 [1024, 8], P(('leaf', 'row'), 'col'), may hold values 0 or 1
- front_rest: float32 [65536, 4096], P(('leaf', 'row'), 'col'), may hold values from -6 to 6
- row_maps: int32 [128, 4], P(('leaf', 'row')), may hold values from 0 to 3, each once within a row
- col_maps: int32 [128, 12], P(('leaf', 'col')), may hold values from 0 to 11, each once within a row
Outputs:
- parent: float32 [32768, 6144], P(('leaf', 'row'), 'col')
The draws below stay inside these ranges and needn't reach their ends.
Inputs may be any that keep to these rules, and one draw needn't show every extreme that they name: `row_maps`: each row is a permutation of 0 to 3. `col_maps`: each row is a permutation of 0 to 11; only its first 8 entries are used.
All inputs are finite; a program needn't handle non-finite values. No bound on the sum of `block_mask` on one device may be relied on, other than what follows from the above.
Results may differ from the reference program's by a relative error of at most 0.0003.
Values sent between devices are 32-bit elements; how exact they have to be, the bound alone decides.
No kernel may reach another device: no remote copies, remote signals or barrier semaphores. Data moves between devices by JAX's collectives and lax.ppermute only.
A program may use at most 64 MiB of HBM per device.

```python
import jax
import jax.numpy as jnp
import numpy as np
from jax import lax

BLK = 128
P_SIZE = 1024
MC = 4096
PC = 6144
WR = 512
WB = 4
PCB = 12
N_LEAF = 32
N_ROW = 4
N_COL = 4


def set_ends(entries, rng, low, high):
    spot = [jax.random.randint(jax.random.fold_in(rng, axis), (), 0, length) for axis, length in enumerate(entries.shape)]
    widest = entries.shape.index(max(entries.shape))
    next_to = spot[:widest] + [(spot[widest] + 1) % entries.shape[widest]] + spot[widest + 1:]
    return entries.at[tuple(spot)].set(low).at[tuple(next_to)].set(high)


def block_scale(rng, extent, split, least, high):
    def one(axis_at, blocks):
        heights = jax.random.uniform(jax.random.fold_in(jax.random.fold_in(rng, 6), axis_at), (blocks,), jnp.float32, least / len(split), high / len(split))
        return jnp.repeat(jnp.exp(heights), extent[axis_at] // blocks).reshape((-1,) + (1,) * (len(extent) - axis_at - 1))

    factor_of = one(*split[0])
    for cut in split[1:]:
        factor_of = factor_of * one(*cut)
    return factor_of


def scatter_about(own_key, shape, deviation, bound, shards=(), held_as=jnp.bfloat16):
    loudness = block_scale(own_key, shape, shards, -0.22, 0.18) if shards else 1.0
    values = jax.random.normal(own_key, shape, jnp.float32) * deviation * loudness
    return jnp.minimum(jnp.maximum(values, -bound), bound).astype(held_as)


def setup_inputs(seed: int = 0) -> dict:
    arg_keys = jax.random.split(jax.random.key(seed), 6)
    return {
        "panel": scatter_about(arg_keys[0], (N_LEAF * MC, P_SIZE), 0.18, 1.2, ((0, 128), (1, 4)), jnp.float32),
        "block_mask": set_ends((jax.random.randint(arg_keys[1], (N_LEAF * MC // BLK, P_SIZE // BLK), 0, 4) < 3).astype(jnp.int32), jax.random.fold_in(arg_keys[1], 1), 0, 1),
        "front_rest": scatter_about(arg_keys[2], (N_LEAF * N_ROW * WR, MC), 1.0, 6.0, ((0, 128), (1, 4)), jnp.float32),
        "row_maps": jax.vmap(lambda own: jax.random.permutation(own, WB))(jax.random.split(arg_keys[3], (N_LEAF * N_ROW))).reshape((N_LEAF * N_ROW, WB)).astype(jnp.int32),
        "col_maps": jax.vmap(lambda own: jax.random.permutation(own, PCB))(jax.random.split(arg_keys[4], (N_LEAF * N_COL))).reshape((N_LEAF * N_COL, PCB)).astype(jnp.int32),
    }


def reference(panel, block_mask, front_rest, row_maps, col_maps):
    halfway = N_LEAF // 2
    win_blocks = WR // BLK
    child_blocks = MC // (BLK * N_COL)
    parent_blocks = PC // (BLK * N_COL)

    def one_child(leaf):
        leaf = leaf.astype(jnp.int32)
        rows = lax.dynamic_slice_in_dim(panel, leaf * MC, MC, 0)
        flags = lax.dynamic_slice_in_dim(block_mask, leaf * (MC // BLK), MC // BLK, 0).astype(jnp.float32)
        masked = (rows.reshape(MC // BLK, BLK, P_SIZE // BLK, BLK) * flags[:, None, :, None]).reshape(MC, P_SIZE)
        window = masked.reshape(N_ROW, MC // N_ROW, P_SIZE)[:, :WR].reshape(N_ROW * WR, P_SIZE)
        front = lax.dynamic_slice_in_dim(front_rest, leaf * (N_ROW * WR), N_ROW * WR, 0)
        update = front - jnp.dot(window, masked.T, precision=lax.Precision.HIGHEST, preferred_element_type=jnp.float32)
        rmaps = lax.dynamic_slice_in_dim(row_maps, leaf * N_ROW, N_ROW, 0)
        cmaps = lax.dynamic_slice_in_dim(col_maps, leaf * N_COL, N_COL, 0)[:, :child_blocks]
        blocks = update.reshape(N_ROW, win_blocks, BLK, N_COL, child_blocks, BLK).transpose(0, 1, 3, 4, 2, 5)
        grid_rows = jnp.arange(N_ROW, dtype=jnp.int32)[:, None, None, None]
        grid_cols = jnp.arange(N_COL, dtype=jnp.int32)[None, None, :, None]
        spread = jnp.zeros((N_ROW, win_blocks, N_COL, parent_blocks, BLK, BLK), jnp.float32)
        return spread.at[grid_rows, rmaps[:, :, None, None], grid_cols, cmaps[None, None, :, :]].set(blocks)

    spread_all = lax.map(one_child, jnp.arange(N_LEAF, dtype=jnp.int32))
    partner = np.arange(N_LEAF) ^ halfway
    summed = spread_all + spread_all[partner]
    summed = summed.reshape(N_LEAF, N_ROW, 2, win_blocks // 2, N_COL, parent_blocks, BLK, BLK)
    upper = (np.arange(N_LEAF) // halfway) % 2
    kept = summed[np.arange(N_LEAF), :, upper]
    return kept.transpose(0, 1, 2, 5, 3, 4, 6).reshape(N_LEAF * N_ROW * WR // 2, PC)
```

```python
import functools

import jax
import jax.numpy as jnp
from jax import lax
from jax.experimental import pallas as pl
from jax.experimental.pallas import tpu as pltpu
from jax.sharding import PartitionSpec as P

BLK = 128
PC = 6144
F32 = jnp.float32
BF16 = jnp.bfloat16
VMEM = pl.BlockSpec(memory_space=pltpu.VMEM)
ANY = pl.BlockSpec(memory_space=pl.ANY)
SMEM = pl.BlockSpec(memory_space=pltpu.SMEM)
LIMIT = 16 * 1024 * 1024


def cost(us):
    return pl.CostEstimate(flops=int(us * 1e9), bytes_accessed=int(us * 2e6), transcendentals=0)


def shift(value, axis, by):
    size = lax.axis_size(axis)
    return lax.ppermute(value, axis, [(i, (i + by) % size) for i in range(size)])


def mask_kernel(flags_ref, panel_ref, out_ref, window_ref):
    for i in range(out_ref.shape[0] // BLK):
        for k in range(out_ref.shape[1] // BLK):
            rows, columns = pl.ds(i * BLK, BLK), pl.ds(k * BLK, BLK)
            value = panel_ref[rows, columns] * flags_ref[k, i].astype(F32)
            out_ref[rows, columns] = value
            if i * BLK < window_ref.shape[0]:
                window_ref[rows, columns] = value


def mask_rows(block_mask, panel, win_rows):
    half = jax.ShapeDtypeStruct((win_rows, panel.shape[1]), F32)
    return pl.pallas_call(
        mask_kernel,
        out_shape=[jax.ShapeDtypeStruct(panel.shape, F32), half],
        in_specs=[SMEM, VMEM],
        out_specs=[VMEM] * 2,
        compiler_params=pltpu.CompilerParams(vmem_limit_bytes=LIMIT),
        cost_estimate=cost(1.5),
    )(block_mask.T, panel)


def after_all(value, *others):
    return lax.optimization_barrier((value, *others))[0]


def halves(value):
    high = value.astype(BF16)
    return high, (value - high.astype(F32)).astype(BF16)


def window_kernel(groups, to_ref, *refs):
    pieces, (high_ref, low_ref) = refs[:-2], refs[-2:]
    for d in range(groups):
        per = len(pieces) // groups
        j = 0
        for piece in pieces[d * per : (d + 1) * per]:
            for i in range(piece.shape[0] // BLK):
                at = pl.ds(pl.multiple_of(to_ref[j] * BLK, BLK), BLK)
                high_ref[d, at], low_ref[d, at] = halves(piece[pl.ds(i * BLK, BLK)])
                j += 1


def split_window(to, groups, *pieces):
    rows = sum(p.shape[0] for p in pieces) // groups
    out = jax.ShapeDtypeStruct((groups, rows, pieces[0].shape[1]), BF16)
    return pl.pallas_call(
        functools.partial(window_kernel, groups),
        out_shape=[out, out],
        in_specs=[SMEM] + [VMEM] * len(pieces),
        out_specs=[VMEM, VMEM],
        compiler_params=pltpu.CompilerParams(vmem_limit_bytes=LIMIT),
        cost_estimate=cost(0.4 * groups),
    )(to, *pieces)


def update_kernel(counts, firsts, quarter_ref, from_ref, place_ref, near_high, near_low, far_high, far_low, front_ref, *refs):
    (big_ref, small_ref), refs = refs[-2:], refs[:-2]
    pieces, outs = refs[: sum(map(len, counts))], refs[sum(map(len, counts)) :]
    rows, width = outs[0].shape[0], outs[0].shape[1] // len(counts)
    first, span = firsts[0] * BLK, rows * len(outs)
    near = near_high.shape[0]
    for q, parts in enumerate(counts):
        k = 0
        for count in parts:
            piece, pieces = pieces[0], pieces[1:]
            for i in range(count):
                big_ref[q, k], small_ref[q, k] = halves(piece[i])
                k += 1
        total = None
        for d in range(near + 1):
            high, low, e = (near_high, near_low, d) if d < near else (far_high, far_low, 0)
            ph, plo = big_ref[q, place_ref[d]], small_ref[q, place_ref[d]]
            for left, right in ((high, ph), (high, plo), (low, ph)):
                term = lax.dot_general(
                    left[e, pl.ds(first, span)], right, (((1,), (1,)), ((), ())), preferred_element_type=F32
                )
                total = term if total is None else total + term
        columns = pl.ds(pl.multiple_of(quarter_ref[q] * width, width), width)
        for o, out_ref in enumerate(outs):
            for i in range(rows // BLK):
                source = pl.ds(pl.multiple_of(from_ref[firsts[o] + i] * BLK, BLK), BLK)
                at = o * rows + i * BLK
                out_ref[pl.ds(i * BLK, BLK), pl.ds(q * width, width)] = (
                    front_ref[source, columns] - total[at : at + BLK]
                )


def update(quarters, sources, place, window, front, groups, firsts, us):
    counts = tuple(tuple(p.shape[0] for p in group) for group in groups)
    pieces = [p for group in groups for p in group]
    out = jax.ShapeDtypeStruct((front.shape[0] // 2, len(groups) * pieces[0].shape[1]), F32)
    return pl.pallas_call(
        functools.partial(update_kernel, counts, firsts),
        out_shape=[out] * len(firsts),
        in_specs=[SMEM] * 3 + [VMEM] * (5 + len(pieces)),
        out_specs=[VMEM] * len(firsts),
        scratch_shapes=[pltpu.VMEM((len(groups), sum(counts[0]), *pieces[0].shape[1:]), BF16)] * 2,
        compiler_params=pltpu.CompilerParams(vmem_limit_bytes=LIMIT),
        cost_estimate=cost(us),
    )(quarters, sources, place, *window, front, *pieces)


def place_kernel(count, mine_ref, other_ref, *refs):
    values, out_ref = refs[:-1], refs[-1]
    out_ref[...] = jnp.zeros_like(out_ref)
    for i, value_ref in enumerate(values):
        maps_ref = mine_ref if i < count else other_ref
        start = sum(v.shape[1] for v in values[:i]) if i < count else sum(v.shape[1] for v in values[count:i])
        for j in range(value_ref.shape[1] // BLK):
            at = pl.ds(pl.multiple_of(maps_ref[start // BLK + j] * BLK, BLK), BLK)
            value = value_ref[:, j * BLK : (j + 1) * BLK]
            out_ref[:, at] = value if i < count else out_ref[:, at] + value


def place_blocks(mine, other, own, got, columns):
    return pl.pallas_call(
        functools.partial(place_kernel, len(own)),
        out_shape=jax.ShapeDtypeStruct((own[0].shape[0], columns), F32),
        in_specs=[SMEM] * 2 + [VMEM] * (len(own) + len(got)),
        out_specs=VMEM,
        compiler_params=pltpu.CompilerParams(vmem_limit_bytes=LIMIT),
        cost_estimate=cost(2),
    )(mine, other, *own, *got)


def add_kernel(slots_ref, value_ref, sum_ref, out_ref):
    out_ref[...] = sum_ref[...] + value_ref[...]


def add_blocks(slots, value, total):
    rows = value.shape[0]
    placed = pl.BlockSpec((rows, BLK), lambda i, s: (0, s[i]))
    return pl.pallas_call(
        add_kernel,
        grid_spec=pltpu.PrefetchScalarGridSpec(
            num_scalar_prefetch=1,
            grid=(value.shape[1] // BLK,),
            in_specs=[pl.BlockSpec((rows, BLK), lambda i, s: (0, i)), placed],
            out_specs=placed,
        ),
        out_shape=jax.ShapeDtypeStruct(total.shape, F32),
        input_output_aliases={2: 0},
        compiler_params=pltpu.CompilerParams(vmem_limit_bytes=LIMIT),
        cost_estimate=cost(1),
    )(slots, value, total)


def body(panel, block_mask, front_rest, row_maps, col_maps):
    n_leaf, n_row, n_col = (lax.axis_size(a) for a in ("leaf", "row", "col"))
    row, col = lax.axis_index("row"), lax.axis_index("col")
    upper = lax.axis_index("leaf") // (n_leaf // 2) % 2
    win_rows, width = front_rest.shape[0], panel.shape[1]
    columns = panel.shape[0] // n_row
    pairs = [(i, i ^ (n_leaf // 2)) for i in range(n_leaf)]
    to_sibling = lambda v: lax.ppermute(v, "leaf", pairs)

    masked, window = mask_rows(block_mask, panel, win_rows)
    other_maps = to_sibling(col_maps)
    by_row = lax.all_to_all(masked, "row", 0, 0, tiled=True)
    by_row = after_all(by_row, other_maps)
    mine = lax.all_to_all(by_row, "col", 0, 0, tiled=True).reshape(n_col, columns, width)
    half = win_rows // 2
    before, after = shift(window, "col", 1), shift(window, "col", -1)
    far_low, far_high = shift(before[:half], "col", 1), shift(after[half:], "col", -1)
    q_before, q_after = shift(mine, "row", 1), shift(mine, "row", -1)
    q_low, q_high = shift(q_before[: n_col // 2], "row", 1), shift(q_after[n_col // 2 :], "row", -1)

    target = row_maps[0]
    to = jnp.where(target // 2 == upper, target % 2, 2 + target % 2).astype(jnp.int32)
    sources = jnp.sum(
        jnp.where(to[None, :] == jnp.arange(to.shape[0])[:, None], jnp.arange(to.shape[0])[None, :], 0), 1
    ).astype(jnp.int32)
    place = jnp.stack([col, (col + n_col - 1) % n_col, (col + 1) % n_col, (col + 2) % n_col]).astype(jnp.int32)
    window = (*split_window(to, 3, window, before, after), *split_window(after_all(to, q_before, q_after), 1, far_low, far_high))

    quarters = jnp.stack([row, (row + n_row - 1) % n_row, (row + 1) % n_row, (row + 2) % n_row]).astype(jnp.int32)
    half = win_rows // BLK // 2
    keep0, send0 = update(quarters[:1], sources, place, window, front_rest, ((mine,),), (0, half), 1.6)
    got0 = to_sibling(send0)
    keep1, send1 = update(quarters[1:3], sources, place, window, front_rest, ((q_before,), (q_after,)), (0, half), 3.2)
    got1 = to_sibling(send1)
    last = ((q_low, q_high),)
    (send2,) = update(quarters[3:], sources, place, window, front_rest, last, (half,), 1)
    got2 = to_sibling(send2)
    (keep2,) = update(quarters[3:], sources, place, window, front_rest, last, (0,), 1)

    per = columns // BLK
    order = (quarters[:, None] * per + jnp.arange(per)[None, :]).reshape(-1)
    pick = (order[:, None] == jnp.arange(n_row * per)[None, :]).astype(jnp.int32)
    slots, other_slots = (jnp.sum(pick * m[:, : n_row * per], 1) for m in (col_maps, other_maps))
    total = place_blocks(slots, other_slots, (keep0, keep1, keep2), (got0, got1), PC // n_col)
    return add_blocks(other_slots[3 * per :], got2, total)


def solution(mesh):
    return jax.shard_map(
        body,
        mesh=mesh,
        in_specs=(
            P(("leaf", "row"), "col"),
            P(("leaf", "row"), "col"),
            P(("leaf", "row"), "col"),
            P(("leaf", "row"), None),
            P(("leaf", "col"), None),
        ),
        out_specs=P(("leaf", "row"), "col"),
        check_vma=False,
    )
```

```python
import functools

import jax
import jax.numpy as jnp
from jax import lax
from jax.experimental import pallas as pl
from jax.experimental.pallas import tpu as pltpu
from jax.sharding import PartitionSpec as P

BLK = 128
PC = 6144
F32 = jnp.float32
BF16 = jnp.bfloat16
VMEM = pl.BlockSpec(memory_space=pltpu.VMEM)
ANY = pl.BlockSpec(memory_space=pl.ANY)
SMEM = pl.BlockSpec(memory_space=pltpu.SMEM)
LIMIT = 16 * 1024 * 1024


def cost(us):
    return pl.CostEstimate(flops=int(us * 1e9), bytes_accessed=int(us * 2e6), transcendentals=0)


def shift(value, axis, by):
    size = lax.axis_size(axis)
    return lax.ppermute(value, axis, [(i, (i + by) % size) for i in range(size)])


def mask_kernel(flags_ref, panel_ref, out_ref, window_ref):
    for i in range(out_ref.shape[0] // BLK):
        for k in range(out_ref.shape[1] // BLK):
            rows, columns = pl.ds(i * BLK, BLK), pl.ds(k * BLK, BLK)
            value = panel_ref[rows, columns] * flags_ref[k, i].astype(F32)
            out_ref[rows, columns] = value
            if i * BLK < window_ref.shape[0]:
                window_ref[rows, columns] = value


def mask_rows(block_mask, panel, win_rows):
    half = jax.ShapeDtypeStruct((win_rows, panel.shape[1]), F32)
    return pl.pallas_call(
        mask_kernel,
        out_shape=[jax.ShapeDtypeStruct(panel.shape, F32), half],
        in_specs=[SMEM, VMEM],
        out_specs=[VMEM] * 2,
        compiler_params=pltpu.CompilerParams(vmem_limit_bytes=LIMIT),
        cost_estimate=cost(1.5),
    )(block_mask.T, panel)


def after_all(value, *others):
    return lax.optimization_barrier((value, *others))[0]


def halves(value):
    high = value.astype(BF16)
    return high, (value - high.astype(F32)).astype(BF16)


def window_kernel(groups, count, to_ref, *refs):
    pieces, (high_ref, low_ref), extra = refs[:count], refs[count : count + 2], refs[count + 2 :]
    for d in range(groups):
        per = count // groups
        j = 0
        for piece in pieces[d * per : (d + 1) * per]:
            for i in range(piece.shape[0] // BLK):
                at = pl.ds(pl.multiple_of(to_ref[j] * BLK, BLK), BLK)
                high_ref[d, at], low_ref[d, at] = halves(piece[pl.ds(i * BLK, BLK)])
                j += 1
    if extra:
        first_ref, second_ref = extra
        rows = first_ref.shape[0]
        first_ref[...] = pieces[1][pl.ds(0, rows)]
        second_ref[...] = pieces[2][pl.ds(rows, rows)]


def split_window(to, groups, us, *pieces, forward=False):
    rows, width = sum(p.shape[0] for p in pieces) // groups, pieces[0].shape[1]
    out = [jax.ShapeDtypeStruct((groups, rows, width), BF16)] * 2
    if forward:
        out += [jax.ShapeDtypeStruct((rows // 2, width), F32)] * 2
    return pl.pallas_call(
        functools.partial(window_kernel, groups, len(pieces)),
        out_shape=out,
        in_specs=[SMEM] + [VMEM] * len(pieces),
        out_specs=[VMEM] * len(out),
        compiler_params=pltpu.CompilerParams(vmem_limit_bytes=LIMIT),
        cost_estimate=cost(us),
    )(to, *pieces)


def update_kernel(counts, firsts, extra, quarter_ref, from_ref, place_ref, near_high, near_low, far_high, far_low, front_ref, *refs):
    (big_ref, small_ref), refs = refs[-2:], refs[:-2]
    if extra:
        extra_ref, refs = refs[0], refs[1:]
    pieces, outs = refs[: sum(map(len, counts))], refs[sum(map(len, counts)) :]
    rows, width = front_ref.shape[0] // 2, outs[0].shape[1] // len(counts)
    if extra:
        outs[0][pl.ds(rows, extra)] = extra_ref[...]
    first, span = firsts[0] * BLK, rows * len(outs)
    near = near_high.shape[0]
    for q, parts in enumerate(counts):
        k = 0
        for count in parts:
            piece, pieces = pieces[0], pieces[1:]
            for i in range(count):
                big_ref[q, k], small_ref[q, k] = halves(piece[i])
                k += 1
        total = None
        for d in range(near + 1):
            high, low, e = (near_high, near_low, d) if d < near else (far_high, far_low, 0)
            ph, plo = big_ref[q, place_ref[d]], small_ref[q, place_ref[d]]
            for left, right in ((high, ph), (high, plo), (low, ph)):
                term = lax.dot_general(
                    left[e, pl.ds(first, span)], right, (((1,), (1,)), ((), ())), preferred_element_type=F32
                )
                total = term if total is None else total + term
        columns = pl.ds(pl.multiple_of(quarter_ref[q] * width, width), width)
        for o, out_ref in enumerate(outs):
            for i in range(rows // BLK):
                source = pl.ds(pl.multiple_of(from_ref[firsts[o] + i] * BLK, BLK), BLK)
                at = o * rows + i * BLK
                out_ref[pl.ds(i * BLK, BLK), pl.ds(q * width, width)] = (
                    front_ref[source, columns] - total[at : at + BLK]
                )


def update(quarters, sources, place, window, front, groups, firsts, us, *extra):
    counts = tuple(tuple(p.shape[0] for p in group) for group in groups)
    pieces = [p for group in groups for p in group]
    more = sum(e.shape[0] for e in extra)
    out = jax.ShapeDtypeStruct((front.shape[0] // 2 + more, len(groups) * pieces[0].shape[1]), F32)
    return pl.pallas_call(
        functools.partial(update_kernel, counts, firsts, more),
        out_shape=[out] * len(firsts),
        in_specs=[SMEM] * 3 + [VMEM] * (5 + len(extra) + len(pieces)),
        out_specs=[VMEM] * len(firsts),
        scratch_shapes=[pltpu.VMEM((len(groups), sum(counts[0]), *pieces[0].shape[1:]), BF16)] * 2,
        compiler_params=pltpu.CompilerParams(vmem_limit_bytes=LIMIT),
        cost_estimate=cost(us),
    )(quarters, sources, place, *window, front, *extra, *pieces)


def place_kernel(count, mine_ref, other_ref, *refs):
    values, out_ref = refs[:-1], refs[-1]
    out_ref[...] = jnp.zeros_like(out_ref)
    for i, value_ref in enumerate(values):
        maps_ref = mine_ref if i < count else other_ref
        start = sum(v.shape[1] for v in values[:i]) if i < count else sum(v.shape[1] for v in values[count:i])
        for j in range(value_ref.shape[1] // BLK):
            at = pl.ds(pl.multiple_of(maps_ref[start // BLK + j] * BLK, BLK), BLK)
            value = value_ref[pl.ds(0, out_ref.shape[0]), j * BLK : (j + 1) * BLK]
            out_ref[:, at] = value if i < count else out_ref[:, at] + value


def place_blocks(mine, other, own, got, columns):
    return pl.pallas_call(
        functools.partial(place_kernel, len(own)),
        out_shape=jax.ShapeDtypeStruct((own[0].shape[0], columns), F32),
        in_specs=[SMEM] * 2 + [VMEM] * (len(own) + len(got)),
        out_specs=VMEM,
        compiler_params=pltpu.CompilerParams(vmem_limit_bytes=LIMIT),
        cost_estimate=cost(2),
    )(mine, other, *own, *got)


def add_kernel(slots_ref, value_ref, sum_ref, out_ref):
    out_ref[...] = sum_ref[...] + value_ref[...]


def add_blocks(slots, value, total):
    rows = value.shape[0]
    placed = pl.BlockSpec((rows, BLK), lambda i, s: (0, s[i]))
    return pl.pallas_call(
        add_kernel,
        grid_spec=pltpu.PrefetchScalarGridSpec(
            num_scalar_prefetch=1,
            grid=(value.shape[1] // BLK,),
            in_specs=[pl.BlockSpec((rows, BLK), lambda i, s: (0, i)), placed],
            out_specs=placed,
        ),
        out_shape=jax.ShapeDtypeStruct(total.shape, F32),
        input_output_aliases={2: 0},
        compiler_params=pltpu.CompilerParams(vmem_limit_bytes=LIMIT),
        cost_estimate=cost(1),
    )(slots, value, total)


def body(panel, block_mask, front_rest, row_maps, col_maps):
    n_leaf, n_row, n_col = (lax.axis_size(a) for a in ("leaf", "row", "col"))
    row, col = lax.axis_index("row"), lax.axis_index("col")
    upper = lax.axis_index("leaf") // (n_leaf // 2) % 2
    win_rows, width = front_rest.shape[0], panel.shape[1]
    columns = panel.shape[0] // n_row
    pairs = [(i, i ^ (n_leaf // 2)) for i in range(n_leaf)]
    to_sibling = lambda v: lax.ppermute(v, "leaf", pairs)

    masked, window = mask_rows(block_mask, panel, win_rows)
    by_row = lax.all_to_all(masked, "row", 0, 0, tiled=True)
    mine = lax.all_to_all(by_row, "col", 0, 0, tiled=True).reshape(n_col, columns, width)
    before, after = shift(window, "col", 1), shift(window, "col", -1)
    target = row_maps[0]
    to = jnp.where(target // 2 == upper, target % 2, 2 + target % 2).astype(jnp.int32)
    sources = jnp.sum(
        jnp.where(to[None, :] == jnp.arange(to.shape[0])[:, None], jnp.arange(to.shape[0])[None, :], 0), 1
    ).astype(jnp.int32)
    *near, low, high = split_window(to, 3, 60, window, before, after, forward=True)
    mine = after_all(mine, low)
    far_low, far_high = shift(low, "col", 1), shift(high, "col", -1)
    lower, upper_half = mine[: n_col // 2], mine[n_col // 2 :]
    b_low, a_high = shift(lower, "row", 1), shift(upper_half, "row", -1)
    b_high, a_low = shift(upper_half, "row", 1), shift(lower, "row", -1)
    q_low, q_high = shift(b_low, "row", 1), shift(a_high, "row", -1)

    place = jnp.stack([col, (col + n_col - 1) % n_col, (col + 1) % n_col, (col + 2) % n_col]).astype(jnp.int32)
    window = (*near, *split_window(after_all(to, b_low, a_high), 1, 0.5, far_low, far_high))

    quarters = jnp.stack([row, (row + n_row - 1) % n_row, (row + 1) % n_row, (row + 2) % n_row]).astype(jnp.int32)
    half = win_rows // BLK // 2
    maps_rows = jnp.pad(col_maps.astype(F32), ((0, 7), (0, columns - col_maps.shape[1])))
    (send0,) = update(quarters[:1], sources, place, window, front_rest, ((mine,),), (half,), 1, maps_rows)
    got0 = to_sibling(send0)
    pair, last = ((b_low, b_high), (a_low, a_high)), ((q_low, q_high),)
    (send1,) = update(after_all(quarters[1:3], send0), sources, place, window, front_rest, pair, (half,), 2)
    got1 = to_sibling(send1)
    (send2,) = update(quarters[3:], sources, place, window, front_rest, last, (half,), 1)
    got2 = to_sibling(send2)
    (keep,) = update(after_all(quarters, send2), sources, place, window, front_rest, ((mine,), *pair, *last), (0,), 4)
    got0 = after_all(got0, keep)
    other_maps = got0[-8:-7, : col_maps.shape[1]].astype(jnp.int32)

    per = columns // BLK
    order = (quarters[:, None] * per + jnp.arange(per)[None, :]).reshape(-1)
    pick = (order[:, None] == jnp.arange(n_row * per)[None, :]).astype(jnp.int32)
    slots, other_slots = (jnp.sum(pick * m[:, : n_row * per], 1) for m in (col_maps, other_maps))
    total = place_blocks(slots, other_slots, (keep,), (got0, got1), PC // n_col)
    return add_blocks(other_slots[3 * per :], got2, total)


def solution(mesh):
    return jax.shard_map(
        body,
        mesh=mesh,
        in_specs=(
            P(("leaf", "row"), "col"),
            P(("leaf", "row"), "col"),
            P(("leaf", "row"), "col"),
            P(("leaf", "row"), None),
            P(("leaf", "col"), None),
        ),
        out_specs=P(("leaf", "row"), "col"),
        check_vma=False,
    )
```

```python
import functools

import jax
import jax.numpy as jnp
from jax import lax
from jax.experimental import pallas as pl
from jax.experimental.pallas import tpu as pltpu
from jax.sharding import PartitionSpec as P

BLK = 128
PC = 6144
F32 = jnp.float32
BF16 = jnp.bfloat16
VMEM = pl.BlockSpec(memory_space=pltpu.VMEM)
ANY = pl.BlockSpec(memory_space=pl.ANY)
SMEM = pl.BlockSpec(memory_space=pltpu.SMEM)
LIMIT = 16 * 1024 * 1024


def cost(us):
    return pl.CostEstimate(flops=int(us * 1e9), bytes_accessed=int(us * 2e6), transcendentals=0)


def shift(value, axis, by):
    size = lax.axis_size(axis)
    return lax.ppermute(value, axis, [(i, (i + by) % size) for i in range(size)])


def mask_kernel(flags_ref, panel_ref, out_ref, window_ref):
    for i in range(out_ref.shape[0] // BLK):
        for k in range(out_ref.shape[1] // BLK):
            rows, columns = pl.ds(i * BLK, BLK), pl.ds(k * BLK, BLK)
            value = panel_ref[rows, columns] * flags_ref[k, i].astype(F32)
            out_ref[rows, columns] = value
            if i * BLK < window_ref.shape[0]:
                window_ref[rows, columns] = value


def mask_rows(block_mask, panel, win_rows):
    half = jax.ShapeDtypeStruct((win_rows, panel.shape[1]), F32)
    return pl.pallas_call(
        mask_kernel,
        out_shape=[jax.ShapeDtypeStruct(panel.shape, F32), half],
        in_specs=[SMEM, VMEM],
        out_specs=[VMEM] * 2,
        compiler_params=pltpu.CompilerParams(vmem_limit_bytes=LIMIT),
        cost_estimate=cost(1.5),
    )(block_mask.T, panel)


def after_all(value, *others):
    return lax.optimization_barrier((value, *others))[0]


def halves(value):
    high = value.astype(BF16)
    return high, (value - high.astype(F32)).astype(BF16)


def window_kernel(groups, count, to_ref, *refs):
    pieces, (high_ref, low_ref), extra = refs[:count], refs[count : count + 2], refs[count + 2 :]
    for d in range(groups):
        per = count // groups
        j = 0
        for piece in pieces[d * per : (d + 1) * per]:
            for i in range(piece.shape[0] // BLK):
                at = pl.ds(pl.multiple_of(to_ref[j] * BLK, BLK), BLK)
                high_ref[d, at], low_ref[d, at] = halves(piece[pl.ds(i * BLK, BLK)])
                j += 1
    if extra:
        first_ref, second_ref = extra
        rows = first_ref.shape[0]
        first_ref[...] = pieces[1][pl.ds(0, rows)]
        second_ref[...] = pieces[2][pl.ds(rows, rows)]


def split_window(to, groups, us, *pieces, forward=False):
    rows, width = sum(p.shape[0] for p in pieces) // groups, pieces[0].shape[1]
    out = [jax.ShapeDtypeStruct((groups, rows, width), BF16)] * 2
    if forward:
        out += [jax.ShapeDtypeStruct((rows // 2, width), F32)] * 2
    return pl.pallas_call(
        functools.partial(window_kernel, groups, len(pieces)),
        out_shape=out,
        in_specs=[SMEM] + [VMEM] * len(pieces),
        out_specs=[VMEM] * len(out),
        compiler_params=pltpu.CompilerParams(vmem_limit_bytes=LIMIT),
        cost_estimate=cost(us),
    )(to, *pieces)


def update_kernel(counts, firsts, extra, quarter_ref, from_ref, place_ref, near_high, near_low, far_high, far_low, front_ref, *refs):
    (big_ref, small_ref), refs = refs[-2:], refs[:-2]
    if extra:
        extra_ref, refs = refs[0], refs[1:]
    pieces, outs = refs[: sum(map(len, counts))], refs[sum(map(len, counts)) :]
    rows, width = front_ref.shape[0] // 2, outs[0].shape[1] // len(counts)
    if extra:
        outs[0][pl.ds(rows, extra)] = extra_ref[...]
    first, span = firsts[0] * BLK, rows * len(outs)
    near = near_high.shape[0]
    for q, parts in enumerate(counts):
        k = 0
        for count in parts:
            piece, pieces = pieces[0], pieces[1:]
            for i in range(count):
                big_ref[q, k], small_ref[q, k] = halves(piece[i])
                k += 1
        total = None
        for d in range(near + 1):
            high, low, e = (near_high, near_low, d) if d < near else (far_high, far_low, 0)
            ph, plo = big_ref[q, place_ref[d]], small_ref[q, place_ref[d]]
            for left, right in ((high, ph), (high, plo), (low, ph)):
                term = lax.dot_general(
                    left[e, pl.ds(first, span)], right, (((1,), (1,)), ((), ())), preferred_element_type=F32
                )
                total = term if total is None else total + term
        columns = pl.ds(pl.multiple_of(quarter_ref[q] * width, width), width)
        for o, out_ref in enumerate(outs):
            for i in range(rows // BLK):
                source = pl.ds(pl.multiple_of(from_ref[firsts[o] + i] * BLK, BLK), BLK)
                at = o * rows + i * BLK
                out_ref[pl.ds(i * BLK, BLK), pl.ds(q * width, width)] = (
                    front_ref[source, columns] - total[at : at + BLK]
                )


def update(quarters, sources, place, window, front, groups, firsts, us, *extra):
    counts = tuple(tuple(p.shape[0] for p in group) for group in groups)
    pieces = [p for group in groups for p in group]
    more = sum(e.shape[0] for e in extra)
    out = jax.ShapeDtypeStruct((front.shape[0] // 2 + more, len(groups) * pieces[0].shape[1]), F32)
    return pl.pallas_call(
        functools.partial(update_kernel, counts, firsts, more),
        out_shape=[out] * len(firsts),
        in_specs=[SMEM] * 3 + [VMEM] * (5 + len(extra) + len(pieces)),
        out_specs=[VMEM] * len(firsts),
        scratch_shapes=[pltpu.VMEM((len(groups), sum(counts[0]), *pieces[0].shape[1:]), BF16)] * 2,
        compiler_params=pltpu.CompilerParams(vmem_limit_bytes=LIMIT),
        cost_estimate=cost(us),
    )(quarters, sources, place, *window, front, *extra, *pieces)


def place_kernel(count, mine_ref, other_ref, *refs):
    values, out_ref = refs[:-1], refs[-1]
    out_ref[...] = jnp.zeros_like(out_ref)
    for i, value_ref in enumerate(values):
        maps_ref = mine_ref if i < count else other_ref
        start = sum(v.shape[1] for v in values[:i]) if i < count else sum(v.shape[1] for v in values[count:i])
        for j in range(value_ref.shape[1] // BLK):
            at = pl.ds(pl.multiple_of(maps_ref[start // BLK + j] * BLK, BLK), BLK)
            value = value_ref[pl.ds(0, out_ref.shape[0]), j * BLK : (j + 1) * BLK]
            out_ref[:, at] = value if i < count else out_ref[:, at] + value


def place_blocks(mine, other, own, got, columns):
    return pl.pallas_call(
        functools.partial(place_kernel, len(own)),
        out_shape=jax.ShapeDtypeStruct((own[0].shape[0], columns), F32),
        in_specs=[SMEM] * 2 + [VMEM] * (len(own) + len(got)),
        out_specs=VMEM,
        compiler_params=pltpu.CompilerParams(vmem_limit_bytes=LIMIT),
        cost_estimate=cost(2),
    )(mine, other, *own, *got)


def add_kernel(slots_ref, value_ref, sum_ref, out_ref):
    out_ref[...] = sum_ref[...] + value_ref[...]


def add_blocks(slots, value, total):
    rows = value.shape[0]
    placed = pl.BlockSpec((rows, BLK), lambda i, s: (0, s[i]))
    return pl.pallas_call(
        add_kernel,
        grid_spec=pltpu.PrefetchScalarGridSpec(
            num_scalar_prefetch=1,
            grid=(value.shape[1] // BLK,),
            in_specs=[pl.BlockSpec((rows, BLK), lambda i, s: (0, i)), placed],
            out_specs=placed,
        ),
        out_shape=jax.ShapeDtypeStruct(total.shape, F32),
        input_output_aliases={2: 0},
        compiler_params=pltpu.CompilerParams(vmem_limit_bytes=LIMIT),
        cost_estimate=cost(1),
    )(slots, value, total)


def body(panel, block_mask, front_rest, row_maps, col_maps):
    n_leaf, n_row, n_col = (lax.axis_size(a) for a in ("leaf", "row", "col"))
    row, col = lax.axis_index("row"), lax.axis_index("col")
    upper = lax.axis_index("leaf") // (n_leaf // 2) % 2
    win_rows, width = front_rest.shape[0], panel.shape[1]
    columns = panel.shape[0] // n_row
    pairs = [(i, i ^ (n_leaf // 2)) for i in range(n_leaf)]
    to_sibling = lambda v: lax.ppermute(v, "leaf", pairs)

    masked, window = mask_rows(block_mask, panel, win_rows)
    by_row = lax.all_to_all(masked, "row", 0, 0, tiled=True)
    mine = lax.all_to_all(by_row, "col", 0, 0, tiled=True).reshape(n_col, columns, width)
    before, after = shift(window, "col", 1), shift(window, "col", -1)
    target = row_maps[0]
    to = jnp.where(target // 2 == upper, target % 2, 2 + target % 2).astype(jnp.int32)
    sources = jnp.sum(
        jnp.where(to[None, :] == jnp.arange(to.shape[0])[:, None], jnp.arange(to.shape[0])[None, :], 0), 1
    ).astype(jnp.int32)
    *near, low, high = split_window(to, 3, 60, window, before, after, forward=True)
    mine = after_all(mine, low)
    low, high = after_all(low, mine), after_all(high, mine)
    far_low, far_high = shift(low, "col", 1), shift(high, "col", -1)
    lower, upper_half = mine[: n_col // 2], mine[n_col // 2 :]
    b_low, a_high = shift(lower, "row", 1), shift(upper_half, "row", -1)
    b_high, a_low = shift(upper_half, "row", 1), shift(lower, "row", -1)
    q_low, q_high = shift(b_low, "row", 1), shift(a_high, "row", -1)

    place = jnp.stack([col, (col + n_col - 1) % n_col, (col + 1) % n_col, (col + 2) % n_col]).astype(jnp.int32)
    window = (*near, *split_window(after_all(to, b_low, a_high), 1, 0.5, far_low, far_high))

    quarters = jnp.stack([row, (row + n_row - 1) % n_row, (row + 1) % n_row, (row + 2) % n_row]).astype(jnp.int32)
    half = win_rows // BLK // 2
    maps_rows = jnp.pad(col_maps.astype(F32), ((0, 7), (0, columns - col_maps.shape[1])))
    (send0,) = update(quarters[:1], sources, place, window, front_rest, ((mine,),), (half,), 1, maps_rows)
    got0 = to_sibling(send0)
    pair, last = ((b_low, b_high), (a_low, a_high)), ((q_low, q_high),)
    (send1,) = update(after_all(quarters[1:3], send0), sources, place, window, front_rest, pair, (half,), 2)
    got1 = to_sibling(send1)
    (send2,) = update(quarters[3:], sources, place, window, front_rest, last, (half,), 1)
    got2 = to_sibling(send2)
    (keep,) = update(after_all(quarters, send2), sources, place, window, front_rest, ((mine,), *pair, *last), (0,), 4)
    got0 = after_all(got0, keep)
    other_maps = got0[-8:-7, : col_maps.shape[1]].astype(jnp.int32)

    per = columns // BLK
    order = (quarters[:, None] * per + jnp.arange(per)[None, :]).reshape(-1)
    pick = (order[:, None] == jnp.arange(n_row * per)[None, :]).astype(jnp.int32)
    slots, other_slots = (jnp.sum(pick * m[:, : n_row * per], 1) for m in (col_maps, other_maps))
    total = place_blocks(slots, other_slots, (keep,), (got0, got1), PC // n_col)
    return add_blocks(other_slots[3 * per :], got2, total)


def solution(mesh):
    return jax.shard_map(
        body,
        mesh=mesh,
        in_specs=(
            P(("leaf", "row"), "col"),
            P(("leaf", "row"), "col"),
            P(("leaf", "row"), "col"),
            P(("leaf", "row"), None),
            P(("leaf", "col"), None),
        ),
        out_specs=P(("leaf", "row"), "col"),
        check_vma=False,
    )
```

```python
import functools

import jax
import jax.numpy as jnp
from jax import lax
from jax.experimental import pallas as pl
from jax.experimental.pallas import tpu as pltpu
from jax.sharding import PartitionSpec as P

BLK = 128
PC = 6144
F32 = jnp.float32
BF16 = jnp.bfloat16
VMEM = pl.BlockSpec(memory_space=pltpu.VMEM)
ANY = pl.BlockSpec(memory_space=pl.ANY)
SMEM = pl.BlockSpec(memory_space=pltpu.SMEM)
LIMIT = 16 * 1024 * 1024


def cost(us):
    return pl.CostEstimate(flops=int(us * 1e9), bytes_accessed=int(us * 2e6), transcendentals=0)


def shift(value, axis, by):
    size = lax.axis_size(axis)
    return lax.ppermute(value, axis, [(i, (i + by) % size) for i in range(size)])


def mask_kernel(flags_ref, panel_ref, out_ref, window_ref):
    for i in range(out_ref.shape[0] // BLK):
        for k in range(out_ref.shape[1] // BLK):
            rows, columns = pl.ds(i * BLK, BLK), pl.ds(k * BLK, BLK)
            value = panel_ref[rows, columns] * flags_ref[k, i].astype(F32)
            out_ref[rows, columns] = value
            if i * BLK < window_ref.shape[0]:
                window_ref[rows, columns] = value


def mask_rows(block_mask, panel, win_rows):
    half = jax.ShapeDtypeStruct((win_rows, panel.shape[1]), F32)
    return pl.pallas_call(
        mask_kernel,
        out_shape=[jax.ShapeDtypeStruct(panel.shape, F32), half],
        in_specs=[SMEM, VMEM],
        out_specs=[VMEM] * 2,
        compiler_params=pltpu.CompilerParams(vmem_limit_bytes=LIMIT),
        cost_estimate=cost(1.5),
    )(block_mask.T, panel)


def after_all(value, *others):
    return lax.optimization_barrier((value, *others))[0]


def halves(value):
    high = value.astype(BF16)
    return high, (value - high.astype(F32)).astype(BF16)


def window_kernel(groups, count, to_ref, *refs):
    pieces, (high_ref, low_ref) = refs[:count], refs[count:]
    for d in range(groups):
        per = count // groups
        j = 0
        for piece in pieces[d * per : (d + 1) * per]:
            for i in range(piece.shape[0] // BLK):
                at = pl.ds(pl.multiple_of(to_ref[j] * BLK, BLK), BLK)
                high_ref[d, at], low_ref[d, at] = halves(piece[pl.ds(i * BLK, BLK)])
                j += 1


def halves_kernel(before_ref, after_ref, low_ref, high_ref):
    rows = low_ref.shape[0]
    low_ref[...] = before_ref[pl.ds(0, rows)]
    high_ref[...] = after_ref[pl.ds(rows, rows)]


def forward_halves(before, after):
    out = jax.ShapeDtypeStruct((before.shape[0] // 2, before.shape[1]), F32)
    return pl.pallas_call(
        halves_kernel,
        out_shape=[out, out],
        in_specs=[VMEM] * 2,
        out_specs=[VMEM] * 2,
        compiler_params=pltpu.CompilerParams(vmem_limit_bytes=LIMIT),
        cost_estimate=cost(0.3),
    )(before, after)


def split_window(to, groups, us, *pieces):
    rows, width = sum(p.shape[0] for p in pieces) // groups, pieces[0].shape[1]
    out = [jax.ShapeDtypeStruct((groups, rows, width), BF16)] * 2
    return pl.pallas_call(
        functools.partial(window_kernel, groups, len(pieces)),
        out_shape=out,
        in_specs=[SMEM] + [VMEM] * len(pieces),
        out_specs=[VMEM] * len(out),
        compiler_params=pltpu.CompilerParams(vmem_limit_bytes=LIMIT),
        cost_estimate=cost(us),
    )(to, *pieces)


def update_kernel(counts, firsts, extra, quarter_ref, from_ref, place_ref, near_high, near_low, far_high, far_low, front_ref, *refs):
    (big_ref, small_ref), refs = refs[-2:], refs[:-2]
    if extra:
        extra_ref, refs = refs[0], refs[1:]
    pieces, outs = refs[: sum(map(len, counts))], refs[sum(map(len, counts)) :]
    rows, width = front_ref.shape[0] // 2, outs[0].shape[1] // len(counts)
    if extra:
        outs[0][pl.ds(rows, extra)] = extra_ref[...]
    first, span = firsts[0] * BLK, rows * len(outs)
    near = near_high.shape[0]
    for q, parts in enumerate(counts):
        k = 0
        for count in parts:
            piece, pieces = pieces[0], pieces[1:]
            for i in range(count):
                big_ref[q, k], small_ref[q, k] = halves(piece[i])
                k += 1
        total = None
        for d in range(near + 1):
            high, low, e = (near_high, near_low, d) if d < near else (far_high, far_low, 0)
            ph, plo = big_ref[q, place_ref[d]], small_ref[q, place_ref[d]]
            for left, right in ((high, ph), (high, plo), (low, ph)):
                term = lax.dot_general(
                    left[e, pl.ds(first, span)], right, (((1,), (1,)), ((), ())), preferred_element_type=F32
                )
                total = term if total is None else total + term
        columns = pl.ds(pl.multiple_of(quarter_ref[q] * width, width), width)
        for o, out_ref in enumerate(outs):
            for i in range(rows // BLK):
                source = pl.ds(pl.multiple_of(from_ref[firsts[o] + i] * BLK, BLK), BLK)
                at = o * rows + i * BLK
                out_ref[pl.ds(i * BLK, BLK), pl.ds(q * width, width)] = (
                    front_ref[source, columns] - total[at : at + BLK]
                )


def update(quarters, sources, place, window, front, groups, firsts, us, *extra):
    counts = tuple(tuple(p.shape[0] for p in group) for group in groups)
    pieces = [p for group in groups for p in group]
    more = sum(e.shape[0] for e in extra)
    out = jax.ShapeDtypeStruct((front.shape[0] // 2 + more, len(groups) * pieces[0].shape[1]), F32)
    return pl.pallas_call(
        functools.partial(update_kernel, counts, firsts, more),
        out_shape=[out] * len(firsts),
        in_specs=[SMEM] * 3 + [VMEM] * (5 + len(extra) + len(pieces)),
        out_specs=[VMEM] * len(firsts),
        scratch_shapes=[pltpu.VMEM((len(groups), sum(counts[0]), *pieces[0].shape[1:]), BF16)] * 2,
        compiler_params=pltpu.CompilerParams(vmem_limit_bytes=LIMIT),
        cost_estimate=cost(us),
    )(quarters, sources, place, *window, front, *extra, *pieces)


def place_kernel(count, mine_ref, other_ref, *refs):
    values, out_ref = refs[:-1], refs[-1]
    out_ref[...] = jnp.zeros_like(out_ref)
    for i, value_ref in enumerate(values):
        maps_ref = mine_ref if i < count else other_ref
        start = sum(v.shape[1] for v in values[:i]) if i < count else sum(v.shape[1] for v in values[count:i])
        for j in range(value_ref.shape[1] // BLK):
            at = pl.ds(pl.multiple_of(maps_ref[start // BLK + j] * BLK, BLK), BLK)
            value = value_ref[pl.ds(0, out_ref.shape[0]), j * BLK : (j + 1) * BLK]
            out_ref[:, at] = value if i < count else out_ref[:, at] + value


def place_blocks(mine, other, own, got, columns):
    return pl.pallas_call(
        functools.partial(place_kernel, len(own)),
        out_shape=jax.ShapeDtypeStruct((own[0].shape[0], columns), F32),
        in_specs=[SMEM] * 2 + [VMEM] * (len(own) + len(got)),
        out_specs=VMEM,
        compiler_params=pltpu.CompilerParams(vmem_limit_bytes=LIMIT),
        cost_estimate=cost(2),
    )(mine, other, *own, *got)


def add_kernel(slots_ref, value_ref, sum_ref, out_ref):
    out_ref[...] = sum_ref[...] + value_ref[...]


def add_blocks(slots, value, total):
    rows = value.shape[0]
    placed = pl.BlockSpec((rows, BLK), lambda i, s: (0, s[i]))
    return pl.pallas_call(
        add_kernel,
        grid_spec=pltpu.PrefetchScalarGridSpec(
            num_scalar_prefetch=1,
            grid=(value.shape[1] // BLK,),
            in_specs=[pl.BlockSpec((rows, BLK), lambda i, s: (0, i)), placed],
            out_specs=placed,
        ),
        out_shape=jax.ShapeDtypeStruct(total.shape, F32),
        input_output_aliases={2: 0},
        compiler_params=pltpu.CompilerParams(vmem_limit_bytes=LIMIT),
        cost_estimate=cost(1),
    )(slots, value, total)


def body(panel, block_mask, front_rest, row_maps, col_maps):
    n_leaf, n_row, n_col = (lax.axis_size(a) for a in ("leaf", "row", "col"))
    row, col = lax.axis_index("row"), lax.axis_index("col")
    upper = lax.axis_index("leaf") // (n_leaf // 2) % 2
    win_rows, width = front_rest.shape[0], panel.shape[1]
    columns = panel.shape[0] // n_row
    pairs = [(i, i ^ (n_leaf // 2)) for i in range(n_leaf)]
    to_sibling = lambda v: lax.ppermute(v, "leaf", pairs)

    masked, window = mask_rows(block_mask, panel, win_rows)
    by_row = lax.all_to_all(masked, "row", 0, 0, tiled=True)
    mine = lax.all_to_all(by_row, "col", 0, 0, tiled=True).reshape(n_col, columns, width)
    before, after = shift(window, "col", 1), shift(window, "col", -1)
    target = row_maps[0]
    to = jnp.where(target // 2 == upper, target % 2, 2 + target % 2).astype(jnp.int32)
    sources = jnp.sum(
        jnp.where(to[None, :] == jnp.arange(to.shape[0])[:, None], jnp.arange(to.shape[0])[None, :], 0), 1
    ).astype(jnp.int32)
    low, high = forward_halves(before, after)
    far_low, far_high = shift(low, "col", 1), shift(high, "col", -1)
    near = split_window(to, 3, 15, window, before, after)
    mine = after_all(mine, *near)
    lower, upper_half = mine[: n_col // 2], mine[n_col // 2 :]
    b_low, a_high = shift(lower, "row", 1), shift(upper_half, "row", -1)
    b_high, a_low = shift(upper_half, "row", 1), shift(lower, "row", -1)
    q_low, q_high = shift(b_low, "row", 1), shift(a_high, "row", -1)

    place = jnp.stack([col, (col + n_col - 1) % n_col, (col + 1) % n_col, (col + 2) % n_col]).astype(jnp.int32)
    window = (*near, *split_window(after_all(to, b_low, a_high), 1, 0.5, far_low, far_high))

    quarters = jnp.stack([row, (row + n_row - 1) % n_row, (row + 1) % n_row, (row + 2) % n_row]).astype(jnp.int32)
    half = win_rows // BLK // 2
    maps_rows = jnp.pad(col_maps.astype(F32), ((0, 7), (0, columns - col_maps.shape[1])))
    (send0,) = update(quarters[:1], sources, place, window, front_rest, ((mine,),), (half,), 1, maps_rows)
    got0 = to_sibling(send0)
    pair, last = ((b_low, b_high), (a_low, a_high)), ((q_low, q_high),)
    (send1,) = update(after_all(quarters[1:3], send0), sources, place, window, front_rest, pair, (half,), 2)
    got1 = to_sibling(send1)
    (send2,) = update(quarters[3:], sources, place, window, front_rest, last, (half,), 1)
    got2 = to_sibling(send2)
    (keep,) = update(after_all(quarters, send2), sources, place, window, front_rest, ((mine,), *pair, *last), (0,), 4)
    got0 = after_all(got0, keep)
    other_maps = got0[-8:-7, : col_maps.shape[1]].astype(jnp.int32)

    per = columns // BLK
    order = (quarters[:, None] * per + jnp.arange(per)[None, :]).reshape(-1)
    pick = (order[:, None] == jnp.arange(n_row * per)[None, :]).astype(jnp.int32)
    slots, other_slots = (jnp.sum(pick * m[:, : n_row * per], 1) for m in (col_maps, other_maps))
    total = place_blocks(slots, other_slots, (keep,), (got0, got1), PC // n_col)
    return add_blocks(other_slots[3 * per :], got2, total)


def solution(mesh):
    return jax.shard_map(
        body,
        mesh=mesh,
        in_specs=(
            P(("leaf", "row"), "col"),
            P(("leaf", "row"), "col"),
            P(("leaf", "row"), "col"),
            P(("leaf", "row"), None),
            P(("leaf", "col"), None),
        ),
        out_specs=P(("leaf", "row"), "col"),
        check_vma=False,
    )
```
